32 devices in a mesh: section: 2 (over core), group: 4 (over y, x), replica: 4 (over z).
Axes of the slice: x: 2, y: 2, z: 4, core: 2. Of those that a mesh axis runs over, the one named last changes fastest.
Arguments:
- tokens: bfloat16 [2, 4096, 768], P(None, ('group', 'replica')), may hold values from -6 to 6
- out_grad: bfloat16 [2, 4096, 768], P(None, ('group', 'replica')), may hold values from -6 to 6
- doc_lengths: int32 [2, 4, 8], P(None, 'group'), may hold values from 1 to 512, 1024 in all within a row
- norm_gain: bfloat16 [2, 768], P('section', 'group'), may hold values from 0.5 to 1.5
- in_weight: bfloat16 [2, 768, 3352], P('section', 'group'), may hold values from -0.21875 to 0.21875
- conv_weight: bfloat16 [2, 1792, 4], P('section', 'group'), may hold values from -3 to 3
- conv_bias: bfloat16 [2, 1792], P('section', 'group'), may hold values from -3 to 3
- dt_bias: bfloat16 [2, 24], P('section', 'group'), may hold values from -7 to -2
- a_log: bfloat16 [2, 24], P('section', 'group'), may hold values from -4.59375 to 0.69921875
- skip_gain: bfloat16 [2, 24], P('section', 'group'), may hold values from 0.5 to 1.5
- out_norm_gain: bfloat16 [2, 1536], P('section', 'group'), may hold values from 0.5 to 1.5
- out_weight: bfloat16 [2, 1536, 768], P('section', 'group'), may hold values from -0.15625 to 0.15625
Outputs:
- section_out: bfloat16 [2, 2, 4096, 768], P('section', None, ('group', 'replica'))
- section_in_grad: float32 [2, 2, 4096, 768], P('section', None, ('group', 'replica'))
- grad_norm_gain: float32 [2, 768], P('section', 'group')
- grad_in_weight: float32 [2, 768, 3352], P('section', 'group')
- grad_conv_weight: float32 [2, 1792, 4], P('section', 'group')
- grad_conv_bias: float32 [2, 1792], P('section', 'group')
- grad_dt_bias: float32 [2, 24], P('section', 'group')
- grad_a_log: float32 [2, 24], P('section', 'group')
- grad_skip_gain: float32 [2, 24], P('section', 'group')
- grad_out_norm_gain: float32 [2, 1536], P('section', 'group')
- grad_out_weight: float32 [2, 1536, 768], P('section', 'group')
The draws below stay inside these ranges and needn't reach their ends.
Inputs may be any that keep to these rules, and one draw needn't show every extreme that they name: `doc_lengths`: each row of 8 lengths sums to 1024; the largest in every row is exactly 512.
All inputs are finite; a program needn't handle non-finite values.
Results may differ from the reference program's by a relative error of at most 0.0094.
Values may be sent and summed in bfloat16 or wider, within the bound.
A program may use at most 256 MiB of HBM per device.

```python
import math
import jax
import jax.numpy as jnp
import numpy as np
from jax import lax

D = 768
H = 24
P_SIZE = 64
N = 128
KW = 4
SPAN = 256
MB = 2
DOCS = 8
INNER = 1536
CONVDIM = 1792
PROJ = 3352
LAYERS = 2
GROUPS = 4
STREAM = 1024
TOKMB = 4096
MAXLEN = 512
N_GROUP = 4


def block_levels(own_key, dims, shards, low, largest):
    factor_of, own = 1.0, jax.random.fold_in(own_key, 6)
    for dim, parts in shards:
        steps = jnp.exp(jax.random.uniform(jax.random.fold_in(own, dim), (parts,), jnp.float32, low / len(shards), largest / len(shards)))
        factor_of = factor_of * jnp.repeat(steps, dims[dim] // parts).reshape([-1 if axis == dim else 1 for axis in range(len(dims))])
    return factor_of


def length_profile(number_of, total, most, slope):
    portions = [(1 << 20) // math.isqrt(grade ** slope) + 1 for grade in range(2, number_of + 1)]
    spare, counts = total - most - (number_of - 1), [1] * (number_of - 1)
    while spare > 0:
        candidates = [i for i in range(number_of - 1) if counts[i] < most]
        pool, budget = sum([portions[i] for i in candidates]), spare
        for i in candidates:
            more = min(most - counts[i], max(1, budget * portions[i] // pool), spare)
            counts[i] = counts[i] + more
            spare = spare - more
    return np.array([most] + counts)


def uneven_parts(key, count, total, reach, skew):
    if count == 2:
        one = jax.random.randint(key, (), max(1, total - reach), min(reach, total - 1) + 1)
        return jnp.stack([one, total - one])
    sizes = jnp.asarray(length_profile(count, total, reach, skew), jnp.int32)
    twos = (count - 1) // 2
    source_of, taker = sizes[1:1 + 2 * twos:2], sizes[2:2 + 2 * twos:2]
    margin = jnp.minimum(source_of - 1, reach - taker)
    moved = jax.random.randint(jax.random.fold_in(key, 1), (twos,), 0, 1 << 20) % (margin + 1)
    sizes = sizes.at[1:1 + 2 * twos:2].set(source_of - moved).at[2:2 + 2 * twos:2].set(taker + moved)
    return sizes[jax.random.permutation(jax.random.fold_in(key, 2), count)]


def bell_draw(rng, extent, spread, most, shards=(), held_as=jnp.bfloat16):
    level = block_levels(rng, extent, shards, -0.22, 0.18) if shards else 1.0
    drawn = jax.random.normal(rng, extent, jnp.float32) * spread * level
    return jnp.minimum(jnp.maximum(drawn, -most), most).astype(held_as)


def setup_inputs(seed: int = 0) -> dict:
    key_list = jax.random.split(jax.random.key(seed), 13)
    return {
        "tokens": bell_draw(key_list[0], (MB, TOKMB, D), 1.0, 6.0, ((1, 16),)),
        "out_grad": bell_draw(key_list[1], (MB, TOKMB, D), 1.0, 6.0, ((1, 16),)),
        "doc_lengths": jax.vmap(lambda own: uneven_parts(own, DOCS, STREAM, MAXLEN, 2))(jax.random.split(key_list[2], MB * GROUPS)).reshape((MB, GROUPS, DOCS)).astype(jnp.int32),
        "norm_gain": jnp.clip(1.0 + 0.1 * jax.random.normal(key_list[3], (LAYERS, D), jnp.float32), 0.5, 1.5).astype(jnp.bfloat16),
        "in_weight": bell_draw(key_list[4], (LAYERS, D, PROJ), D ** -0.5, 0.21875, ((0, 2), (1, 4))),
        "conv_weight": bell_draw(key_list[5], (LAYERS, CONVDIM, KW), KW ** -0.5, 3.0, ((0, 2), (1, 4))),
        "conv_bias": bell_draw(key_list[6], (LAYERS, CONVDIM), 0.5, 3.0, ((0, 2), (1, 4))),
        "dt_bias": jnp.clip(-7.0 + 5.0 * jax.random.uniform(key_list[7], (LAYERS, H), jnp.float32) ** block_levels(key_list[7], (LAYERS, H), ((0, 2), (1, 4)), -0.2, 0.2), -7.0, -2.0).astype(jnp.bfloat16),
        "a_log": jnp.clip(-4.59375 + 5.2929688 * jax.random.uniform(key_list[8], (LAYERS, H), jnp.float32) ** block_levels(key_list[8], (LAYERS, H), ((0, 2), (1, 4)), -0.2, 0.2), -4.59375, 0.69921875).astype(jnp.bfloat16),
        "skip_gain": jnp.clip(0.5 + 1.0 * jax.random.uniform(key_list[9], (LAYERS, H), jnp.float32) ** block_levels(key_list[9], (LAYERS, H), ((0, 2), (1, 4)), -0.2, 0.2), 0.5, 1.5).astype(jnp.bfloat16),
        "out_norm_gain": jnp.clip(1.0 + 0.1 * jax.random.normal(key_list[10], (LAYERS, INNER), jnp.float32), 0.5, 1.5).astype(jnp.bfloat16),
        "out_weight": bell_draw(key_list[11], (LAYERS, INNER, D), INNER ** -0.5, 0.15625, ((0, 2), (1, 4))),
    }


EPSILON = 1e-05
PRECISE = lax.Precision.HIGHEST

@jax.custom_vjp
def low(v):
    return lax.optimization_barrier(v.astype(jnp.bfloat16)).astype(jnp.float32)

@jax.custom_vjp
def low_back(v):
    return v

def low_keep(v):
    return (low(v), None)

def low_pass(kept, grad):
    return (grad,)

def back_keep(v):
    return (v, None)

def back_low(kept, grad):
    return (low(grad),)
low.defvjp(low_keep, low_pass)
low_back.defvjp(back_keep, back_low)

def block_step(memory, block_data):
    inputs, in_basis, out_basis, step_size, log_decay, doc_rows, before = block_data
    length = doc_rows.shape[0]
    cumulate = jnp.cumsum(log_decay, axis=0)
    order_idx = jnp.arange(length)
    allowed = (doc_rows[:, None] == doc_rows[None, :]) & (order_idx[:, None] >= order_idx[None, :])
    by_head = cumulate.T
    spread_log = by_head[:, :, None] - by_head[:, None, :]
    decay_mat = jnp.where(allowed[None], jnp.exp(jnp.where(allowed[None], spread_log, 0.0)), 0.0)
    inner_cb = jnp.dot(out_basis, in_basis.T, precision=PRECISE)
    weight_mat = decay_mat * inner_cb[None] * step_size.T[:, None, :]
    intra_out = jnp.einsum('hts,shp->thp', weight_mat, inputs, precision=PRECISE)
    inflow = (doc_rows == before).astype(jnp.float32)
    inter_out = (jnp.exp(cumulate) * inflow[:, None])[:, :, None] * jnp.einsum('tn,hpn->thp', out_basis, memory, precision=PRECISE)
    last_doc = doc_rows[-1]
    tail_weight = jnp.exp(cumulate[-1][None, :] - cumulate) * (doc_rows == last_doc).astype(jnp.float32)[:, None] * step_size
    fresh_state = jnp.einsum('shp,sn->hpn', tail_weight[:, :, None] * inputs, in_basis, precision=PRECISE)
    carry_scale = (jnp.exp(cumulate[-1]) * (last_doc == before).astype(jnp.float32))[:, None, None]
    return (memory * carry_scale + fresh_state, intra_out + inter_out)

def mixer(values, doc_rows, params):
    gain_in, weight_in_proj, conv_taps, conv_shift, dt_shift, log_rate, skip_part, gain_out, weight_out = params
    length = values.shape[0]
    normed = low(values * lax.rsqrt(lax.optimization_barrier(jnp.mean(values * values, axis=-1, keepdims=True)) + EPSILON) * gain_in[None, :])
    projected = low_back(jnp.dot(normed, weight_in_proj, precision=PRECISE))
    gate_raw = projected[:, :INNER]
    conv_raw = projected[:, INNER:INNER + CONVDIM]
    dt_raw = projected[:, INNER + CONVDIM:]
    extended = jnp.concatenate([jnp.zeros((KW - 1, CONVDIM), jnp.float32), conv_raw], axis=0)
    doc_ext = jnp.concatenate([jnp.full((KW - 1,), -1, jnp.int32), doc_rows], axis=0)
    conv_sum = conv_shift[None, :]
    for offset in range(KW):
        same_doc = (doc_ext[offset:offset + length] == doc_rows).astype(jnp.float32)
        conv_sum = conv_sum + conv_taps[:, offset][None, :] * extended[offset:offset + length] * same_doc[:, None]
    activated = jax.nn.silu(conv_sum)
    inputs = activated[:, :INNER].reshape(length, H, P_SIZE)
    in_basis = activated[:, INNER:INNER + N]
    out_basis = activated[:, INNER + N:]
    step_size = jax.nn.softplus(dt_raw + dt_shift[None, :])
    log_decay = -step_size * jnp.exp(log_rate)[None, :]
    blocks_num = length // SPAN
    befores = jnp.concatenate([jnp.full((1,), -1, jnp.int32), doc_rows[SPAN - 1::SPAN][:-1]], axis=0)
    block_data = (inputs.reshape(blocks_num, SPAN, H, P_SIZE), in_basis.reshape(blocks_num, SPAN, N), out_basis.reshape(blocks_num, SPAN, N), step_size.reshape(blocks_num, SPAN, H), log_decay.reshape(blocks_num, SPAN, H), doc_rows.reshape(blocks_num, SPAN), befores)
    end_state, block_out = lax.scan(jax.checkpoint(block_step), jnp.zeros((H, P_SIZE, N), jnp.float32), block_data)
    mixed_out = block_out.reshape(length, H, P_SIZE) + skip_part[None, :, None] * inputs
    flat_out = mixed_out.reshape(length, INNER)
    gated_out = flat_out * jax.nn.silu(gate_raw)
    result = low(gated_out * lax.rsqrt(lax.optimization_barrier(jnp.mean(gated_out * gated_out, axis=-1, keepdims=True)) + EPSILON) * gain_out[None, :])
    return values + jnp.dot(result, weight_out, precision=PRECISE)

def layer(streams, doc_all, params):

    def one_stream(carry_val, stream_item):
        return (carry_val, mixer(stream_item[0], stream_item[1], params))
    unused_carry, outputs = lax.scan(one_stream, jnp.zeros((), jnp.float32), (streams, doc_all))
    return outputs

def reference(tokens, out_grad, doc_lengths, norm_gain, in_weight, conv_weight, conv_bias, dt_bias, a_log, skip_gain, out_norm_gain, out_weight):
    streams_count = MB * N_GROUP
    values = tokens.astype(jnp.float32).reshape(streams_count, STREAM, D)
    lengths = doc_lengths.reshape(streams_count, DOCS).astype(jnp.int32)
    position = jnp.arange(STREAM, dtype=jnp.int32)
    ends_cum = jnp.cumsum(lengths, axis=1).astype(jnp.int32)
    doc_all = lax.optimization_barrier(jnp.sum((ends_cum[:, None, :] <= position[None, :, None]).astype(jnp.int32), axis=2)).astype(jnp.int32)
    params = [param_item.astype(jnp.float32) for param_item in (norm_gain, in_weight, conv_weight, conv_bias, dt_bias, a_log, skip_gain, out_norm_gain, out_weight)]
    first_set = tuple((param_item[0] for param_item in params))
    second_set = tuple((param_item[1] for param_item in params))
    hidden, back_first = jax.vjp(lambda stream_in, param_set: layer(stream_in, doc_all, param_set), values, first_set)
    hidden_low = low(hidden)
    final_out, back_second = jax.vjp(lambda stream_in, param_set: layer(stream_in, doc_all, param_set), hidden_low, second_set)
    cotangent = out_grad.astype(jnp.float32).reshape(streams_count, STREAM, D)
    grad_hidden, grads_second = back_second(cotangent)
    grad_tokens, grads_first = back_first(low(grad_hidden))
    shape_out = (MB, N_GROUP * STREAM, D)
    section_out = jnp.stack([hidden_low.reshape(shape_out), final_out.reshape(shape_out)]).astype(jnp.bfloat16)
    section_in_grad = jnp.stack([grad_tokens.reshape(shape_out), grad_hidden.reshape(shape_out)])
    grad_list = [jnp.stack([first_grad, second_grad]) for first_grad, second_grad in zip(grads_first, grads_second)]
    return (section_out, section_in_grad, grad_list[0], grad_list[1], grad_list[2], grad_list[3], grad_list[4], grad_list[5], grad_list[6], grad_list[7], grad_list[8])
```

```python
import jax
import jax.numpy as jnp
from jax import lax
from jax.experimental import pallas as pl
from jax.experimental.pallas import tpu as pltpu
from jax.sharding import PartitionSpec as P

H = 24
P_SIZE = 64
N = 128
KW = 4
INNER = 1536
CONVDIM = 1792
PAIRS = H // 2

EPSILON = 1e-05
PRECISE = lax.Precision.HIGHEST
F32 = jnp.float32
BF16 = jnp.bfloat16


def passed_along(block, axis, distance):
    devices = range(lax.axis_size(axis))
    route = [(i - distance, i) for i in devices if i - distance in devices]
    return lax.ppermute(block, axis, route)


def swapped(block):
    return lax.ppermute(block, "section", [(0, 1), (1, 0)])


def doc_index(lengths_row, first_pos, count_rows):
    position = first_pos + jnp.arange(count_rows, dtype=jnp.int32)
    ends_cum = jnp.cumsum(lengths_row)
    counted = jnp.sum((ends_cum[None, :] <= position[:, None]).astype(jnp.int32), axis=1)
    return jnp.where(position < 0, -1, counted)


def dot_nn(a, b):
    return jnp.dot(a.astype(BF16), b.astype(BF16), preferred_element_type=F32)


def dot_nt(a, b):
    return lax.dot_general(
        a.astype(BF16), b.astype(BF16), (((1,), (1,)), ((), ())), preferred_element_type=F32
    )


def dot_tn(a, b):
    return lax.dot_general(
        a.astype(BF16), b.astype(BF16), (((0,), (0,)), ((), ())), preferred_element_type=F32
    )


def allowed_pairs(doc_col, doc_row):
    length = doc_col.shape[0]
    later = lax.broadcasted_iota(jnp.int32, (length, length), 0)
    earlier = lax.broadcasted_iota(jnp.int32, (length, length), 1)
    return (doc_col == doc_row) & (later >= earlier)


def head_decay(cum_ref, cum_t_ref, head):
    cum = cum_ref[...]
    lane = lax.broadcasted_iota(jnp.int32, cum.shape, 1)
    column = jnp.sum(jnp.where(lane == head, cum, 0.0), axis=1, keepdims=True)
    return jnp.exp(jnp.minimum(column - cum_t_ref[pl.ds(head, 1), :], 0.0))


def intra_fwd_kernel(
    x_ref, b_ref, c_ref, cum_ref, cum_t_ref, step_t_ref, dcol_ref, drow_ref, y_ref, cb_ref
):
    pair = pl.program_id(0)

    @pl.when(pair == 0)
    def _():
        allowed = allowed_pairs(dcol_ref[...], drow_ref[...])
        cb_ref[...] = jnp.where(allowed, dot_nt(c_ref[...], b_ref[...]), 0.0)

    parts = []
    for j in range(2):
        head = 2 * pair + j
        decay = head_decay(cum_ref, cum_t_ref, head)
        weights = decay * cb_ref[...] * step_t_ref[pl.ds(head, 1), :]
        parts.append(dot_nn(weights, x_ref[:, j * P_SIZE : (j + 1) * P_SIZE]))
    y_ref[...] = jnp.concatenate(parts, axis=1)


def whole(shape):
    return pl.BlockSpec(shape, lambda i: (0,) * len(shape))


def per_pair(length):
    return pl.BlockSpec((length, 2 * P_SIZE), lambda i: (0, i))


def intra_forward(inputs, in_basis, out_basis, cum, cum_t, step_t, doc_col, doc_row):
    length = inputs.shape[0]
    return pl.pallas_call(
        intra_fwd_kernel,
        grid=(PAIRS,),
        in_specs=[
            per_pair(length),
            whole((length, N)),
            whole((length, N)),
            whole((length, H)),
            whole((H, length)),
            whole((H, length)),
            whole((length, 1)),
            whole((1, length)),
        ],
        out_specs=per_pair(length),
        out_shape=jax.ShapeDtypeStruct((length, INNER), F32),
        scratch_shapes=[pltpu.VMEM((length, length), F32)],
        compiler_params=pltpu.CompilerParams(vmem_limit_bytes=24 << 20),
        cost_estimate=pl.CostEstimate(
            flops=2 * length * length * INNER, bytes_accessed=8 * length * INNER, transcendentals=H * length * length
        ),
    )(inputs, in_basis, out_basis, cum, cum_t, step_t, doc_col, doc_row)


def intra_bwd_kernel(
    x_ref, dy_ref, b_ref, c_ref, cum_ref, cum_t_ref, step_t_ref, dcol_ref, drow_ref,
    dx_ref, rows_ref, cols_ref, db_ref, dc_ref, cb_ref, acc_ref,
):
    pair = pl.program_id(0)

    @pl.when(pair == 0)
    def _():
        allowed = allowed_pairs(dcol_ref[...], drow_ref[...])
        cb_ref[...] = jnp.where(allowed, dot_nt(c_ref[...], b_ref[...]), 0.0)
        acc_ref[...] = jnp.zeros_like(acc_ref)
        rows_ref[...] = jnp.zeros_like(rows_ref)

    parts = []
    for j in range(2):
        head = 2 * pair + j
        span = slice(j * P_SIZE, (j + 1) * P_SIZE)
        step_row = step_t_ref[pl.ds(head, 1), :]
        decay = head_decay(cum_ref, cum_t_ref, head)
        grad_y = dy_ref[:, span]
        cross = dot_nt(grad_y, x_ref[:, span])
        basis = cb_ref[...]
        scaled = decay * step_row
        acc_ref[...] += scaled * cross
        parts.append(dot_tn(scaled * basis, grad_y))
        product = decay * basis * cross
        cols_ref[pl.ds(head, 1), :] = jnp.sum(product, axis=0, keepdims=True)
        row_sum = jnp.sum(product * step_row, axis=1, keepdims=True)
        lane = lax.broadcasted_iota(jnp.int32, rows_ref.shape, 1)
        rows_ref[...] += jnp.where(lane == head, row_sum, 0.0)
    dx_ref[...] = jnp.concatenate(parts, axis=1)

    @pl.when(pair == PAIRS - 1)
    def _():
        allowed = allowed_pairs(dcol_ref[...], drow_ref[...])
        grad_cb = jnp.where(allowed, acc_ref[...], 0.0)
        dc_ref[...] = dot_nn(grad_cb, b_ref[...])
        db_ref[...] = dot_tn(grad_cb, c_ref[...])


def intra_backward(inputs, grad_y, in_basis, out_basis, cum, cum_t, step_t, doc_col, doc_row):
    length = inputs.shape[0]
    return pl.pallas_call(
        intra_bwd_kernel,
        grid=(PAIRS,),
        in_specs=[
            per_pair(length),
            per_pair(length),
            whole((length, N)),
            whole((length, N)),
            whole((length, H)),
            whole((H, length)),
            whole((H, length)),
            whole((length, 1)),
            whole((1, length)),
        ],
        out_specs=[
            per_pair(length),
            whole((length, H)),
            whole((H, length)),
            whole((length, N)),
            whole((length, N)),
        ],
        out_shape=[
            jax.ShapeDtypeStruct((length, INNER), F32),
            jax.ShapeDtypeStruct((length, H), F32),
            jax.ShapeDtypeStruct((H, length), F32),
            jax.ShapeDtypeStruct((length, N), F32),
            jax.ShapeDtypeStruct((length, N), F32),
        ],
        scratch_shapes=[pltpu.VMEM((length, length), F32), pltpu.VMEM((length, length), F32)],
        compiler_params=pltpu.CompilerParams(vmem_limit_bytes=24 << 20),
        cost_estimate=pl.CostEstimate(
            flops=4 * length * length * INNER, bytes_accessed=12 * length * INNER, transcendentals=H * length * length
        ),
    )(inputs, grad_y, in_basis, out_basis, cum, cum_t, step_t, doc_col, doc_row)


def head_map():
    return (jnp.arange(INNER)[None, :] // P_SIZE == jnp.arange(H)[:, None]).astype(F32)


def expand(per_head):
    return jnp.dot(per_head, head_map(), precision=PRECISE)


def head_sum(values):
    return lax.dot_general(
        values, head_map(), (((1,), (1,)), ((), ())), precision=lax.Precision.HIGH
    )


def combine_states(state, passes, reverse):
    count = lax.axis_size("replica")
    place = lax.axis_index("replica")
    gathered = lax.all_gather(state.astype(BF16), "replica")
    factor = jnp.ones((H,), F32)
    weights = [None] * count
    for source in range(count) if reverse else range(count - 1, -1, -1):
        active = (source > place) if reverse else (source < place)
        weights[source] = jnp.where(active, factor, 0.0)
        factor = jnp.where(active, factor * passes[source], factor)
    total = jnp.zeros((H, P_SIZE, N), F32)
    for source in range(count):
        total = total + weights[source][:, None, None] * gathered[source].astype(F32).reshape(
            H, P_SIZE, N
        )
    return total.reshape(INNER, N)


def rms_factor(values):
    return lax.rsqrt(jnp.mean(values * values, axis=-1, keepdims=True) + EPSILON)


def rms_backward(values, factor, gain, grad):
    scaled = grad * gain[None, :]
    grad_gain = jnp.sum(grad * values * factor, axis=0)
    inner = jnp.mean(scaled * values, axis=-1, keepdims=True)
    return factor * scaled - values * (factor * factor * factor * inner), grad_gain


def silu_slope(values):
    gate = jax.nn.sigmoid(values)
    return gate * (1.0 + values * (1.0 - gate))


def forward_layer(layer_in, params, doc_ext):
    gain_in, w_in, taps, shift, dt_shift, log_rate, skip, gain_out, w_out = params
    length = layer_in.shape[0]
    doc_rows = doc_ext[KW - 1 :]
    before = doc_ext[KW - 2]
    values = layer_in.astype(F32)
    normed = (values * rms_factor(values) * gain_in[None, :]).astype(BF16)
    gate_raw = dot_nn(normed, w_in[:, :INNER])
    rest = dot_nn(normed, w_in[:, INNER:])
    conv_raw = rest[:, :CONVDIM]
    dt_raw = rest[:, CONVDIM:]
    rim = passed_along(conv_raw[length - (KW - 1) :], "replica", 1)
    extended = jnp.concatenate([rim, conv_raw], axis=0)
    conv = shift[None, :]
    for k in range(KW):
        same = (doc_ext[k : k + length] == doc_rows).astype(F32)
        conv = conv + taps[:, k][None, :] * extended[k : k + length] * same[:, None]
    act = jax.nn.silu(conv)
    inputs = act[:, :INNER]
    in_basis = act[:, INNER : INNER + N]
    out_basis = act[:, INNER + N :]
    step = jax.nn.softplus(dt_raw + dt_shift[None, :])
    log_decay = -step * jnp.exp(log_rate)[None, :]
    order = jnp.arange(length)
    lower = (order[:, None] >= order[None, :]).astype(F32)
    cum = jnp.dot(lower, log_decay, precision=PRECISE)
    last = cum[-1]
    inflow = (doc_rows == before).astype(F32)
    weight_in = jnp.exp(cum) * inflow[:, None]
    tail = jnp.exp(last[None, :] - cum) * (doc_rows == doc_rows[-1]).astype(F32)[:, None]
    pass_on = jnp.exp(last) * (doc_rows[-1] == before).astype(F32)
    passes = lax.all_gather(pass_on, "replica")
    tail_wide = expand(tail * step)
    state = dot_tn(tail_wide * inputs, in_basis)
    entering = combine_states(state, passes, False)
    kernel_side = (cum, cum.T, step.T, doc_rows[:, None], doc_rows[None, :])
    intra = intra_forward(inputs, in_basis, out_basis, *kernel_side)
    weight_wide = expand(weight_in)
    inter = weight_wide * dot_nt(out_basis, entering)
    skip_wide = jnp.repeat(skip, P_SIZE)
    mixed = intra + skip_wide[None, :] * inputs + inter
    gated = mixed * jax.nn.silu(gate_raw)
    factor = rms_factor(gated)
    result = (gated * factor * gain_out[None, :]).astype(BF16)
    output = (values + dot_nn(result, w_out)).astype(BF16)
    kept = (
        layer_in, normed, gate_raw, dt_raw, extended, conv, act, step, log_decay, tail, pass_on,
        passes, tail_wide, entering, kernel_side, weight_wide, inter, mixed, factor, result,
    )
    return output, kept


def backward_layer(incoming, kept, params, doc_ext, pending):
    gain_in, w_in, taps, shift, dt_shift, log_rate, skip, gain_out, w_out = params
    (
        layer_in, normed, gate_raw, dt_raw, extended, conv, act, step, log_decay, tail, pass_on,
        passes, tail_wide, entering, kernel_side, weight_wide, inter, mixed, factor, result,
    ) = kept
    length = layer_in.shape[0]
    doc_rows = doc_ext[KW - 1 :]
    inputs = act[:, :INNER]
    in_basis = act[:, INNER : INNER + N]
    out_basis = act[:, INNER + N :]
    grad_result = dot_nt(incoming, w_out)
    silu_gate = jax.nn.silu(gate_raw)
    grad_gated, grad_gain_out = rms_backward(mixed * silu_gate, factor, gain_out, grad_result)
    grad_mixed = grad_gated * silu_gate
    weighted = weight_wide * grad_mixed
    grad_entering = dot_tn(weighted, out_basis)
    carried = combine_states(grad_entering, passes, True)
    grad_inputs, row_sums, col_sums, grad_in_basis, grad_out_basis = intra_backward(
        inputs, grad_mixed, in_basis, out_basis, *kernel_side
    )
    grad_out_weight = dot_tn(result, incoming)
    grad_gate = grad_gated * mixed * silu_slope(gate_raw)
    skip_wide = jnp.repeat(skip, P_SIZE)
    grad_skip = jnp.sum(jnp.sum(grad_mixed * inputs, axis=0).reshape(H, P_SIZE), axis=1)
    grad_inflow = head_sum(grad_mixed * inter)
    grad_out_basis = grad_out_basis + dot_nn(weighted, entering)
    grad_pass = jnp.sum((carried * entering).reshape(H, P_SIZE * N), axis=1)
    back_state = dot_nt(in_basis, carried)
    grad_inputs = grad_inputs + skip_wide[None, :] * grad_mixed + tail_wide * back_state
    grad_in_basis = grad_in_basis + dot_nn(tail_wide * inputs, carried)
    grad_tail = head_sum(inputs * back_state)
    by_tail = grad_tail * tail * step
    by_step = col_sums.T
    grad_step = by_step + grad_tail * tail
    grad_cum = row_sums - by_step * step + grad_inflow - by_tail
    grad_last = jnp.sum(by_tail, axis=0) + grad_pass * pass_on
    order = jnp.arange(length)
    upper = (order[:, None] <= order[None, :]).astype(F32)
    grad_log = jnp.dot(upper, grad_cum, precision=PRECISE) + grad_last[None, :]
    grad_step = grad_step - jnp.exp(log_rate)[None, :] * grad_log
    grad_rate = jnp.sum(grad_log * log_decay, axis=0)
    grad_dt = grad_step * jax.nn.sigmoid(dt_raw + dt_shift[None, :])
    grad_bias = jnp.sum(grad_dt, axis=0)
    grad_act = jnp.concatenate([grad_inputs, grad_in_basis, grad_out_basis], axis=1)
    grad_conv = grad_act * silu_slope(conv)
    grad_shift = jnp.sum(grad_conv, axis=0)
    grad_taps = []
    grad_ext = jnp.zeros((length + KW - 1, CONVDIM), F32)
    for k in range(KW):
        same = (doc_ext[k : k + length] == doc_rows).astype(F32)[:, None] * grad_conv
        grad_taps.append(jnp.sum(same * extended[k : k + length], axis=0))
        grad_ext = grad_ext + jnp.pad(
            taps[:, k][None, :] * same, ((k, KW - 1 - k), (0, 0))
        )
    rim_back = passed_along(grad_ext[: KW - 1], "replica", -1)
    grad_raw = grad_ext[KW - 1 :] + jnp.pad(rim_back, ((length - (KW - 1), 0), (0, 0)))
    grad_proj = jnp.concatenate([grad_gate, grad_raw, grad_dt], axis=1).astype(BF16)
    grad_normed = dot_nt(grad_proj, w_in)
    if pending is not None:
        grad_proj, pending = lax.optimization_barrier((grad_proj, pending))
    grad_in_weight = dot_tn(normed, grad_proj)
    values = layer_in.astype(F32)
    grad_values, grad_gain_in = rms_backward(values, rms_factor(values), gain_in, grad_normed)
    grad_input = incoming.astype(F32) + grad_values
    small = (
        grad_gain_in, jnp.stack(grad_taps, axis=1), grad_shift, grad_bias, grad_rate, grad_skip,
        grad_gain_out,
    )
    return grad_input, grad_in_weight, grad_out_weight, small, pending


def packed_halves(w_in, w_out, groups):
    rows = w_in.shape[0] // groups // 2
    pairs = w_out.reshape(groups, 2, 2, rows, w_out.shape[1])
    return jnp.concatenate(
        [pairs[:, :, 0], pairs[:, :, 1], w_in.reshape(groups, 2, rows, w_in.shape[1])], axis=-1
    )


def unpacked(first, second, width):
    full = jnp.stack([first, second], axis=1)
    groups, _, rows, _ = full.shape
    w_in = full[..., 2 * width :].reshape(groups * 2 * rows, -1)
    w_out = jnp.stack([full[..., :width], full[..., width : 2 * width]], axis=2)
    return w_in, w_out.reshape(groups * 4 * rows, width)


def reduce_layer(grad_in, grad_out, section_idx):
    groups = lax.axis_size("group")
    halves = packed_halves(grad_in.astype(BF16), grad_out.astype(BF16), groups)
    away = lax.dynamic_index_in_dim(halves, 1 - section_idx, 1, keepdims=False)
    here = lax.dynamic_index_in_dim(halves, section_idx, 1, keepdims=False)
    both = (here.astype(F32) + swapped(away).astype(F32)).astype(BF16)
    owned = lax.psum_scatter(both, "group", scatter_dimension=0, tiled=False)
    return lax.psum(owned, "replica")


def on_device(
    tokens, out_grad, doc_lengths, norm_gain, in_weight, conv_weight, conv_bias, dt_bias, a_log,
    skip_gain, out_norm_gain, out_weight,
):
    row_count = tokens.shape[1]
    section_idx = lax.axis_index("section")
    at_first = section_idx == 0
    groups = lax.axis_size("group")
    first_pos = lax.axis_index("replica") * row_count - (KW - 1)
    smalls = (norm_gain, conv_weight, conv_bias, dt_bias, a_log, skip_gain, out_norm_gain)

    width = tokens.shape[2]

    own_halves = packed_halves(in_weight[0], out_weight[0], 1)[0]
    keep = lax.dynamic_index_in_dim(own_halves, section_idx, 0, keepdims=False)
    got = swapped(lax.dynamic_index_in_dim(own_halves, 1 - section_idx, 0, keepdims=False))
    half_first = jnp.where(at_first, keep, got)
    half_second = jnp.where(at_first, got, keep)

    packed = jnp.concatenate([item.reshape(-1) for item in smalls])
    small_own = lax.all_gather(packed, "group")
    small_got = swapped(small_own)
    small_all = jnp.stack(
        [jnp.where(at_first, small_own, small_got), jnp.where(at_first, small_got, small_own)]
    )

    gathered_first = lax.all_gather(half_first, "group")
    gathered_first, half_second = lax.optimization_barrier((gathered_first, half_second))
    weights = []
    for mine in (gathered_first, lax.all_gather(half_second, "group")):
        other = swapped(mine)
        weights.append(
            unpacked(jnp.where(at_first, mine, other), jnp.where(at_first, other, mine), width)
        )
    w_in = (weights[0][0], weights[1][0])
    w_out = (weights[0][1], weights[1][1])
    layer_params = []
    for layer in range(2):
        pieces = []
        start = 0
        for item in smalls:
            size = item.size
            piece = small_all[layer, :, start : start + size].astype(F32)
            pieces.append(piece.reshape((groups * item.shape[1],) + item.shape[2:]))
            start += size
        layer_params.append(
            (pieces[0], w_in[layer]) + tuple(pieces[1:]) + (w_out[layer],)
        )

    lengths_row = lax.dynamic_index_in_dim(doc_lengths[:, 0, :], section_idx, 0, keepdims=False)
    doc_ext = doc_index(lengths_row, first_pos, row_count + KW - 1)
    own_tokens = lax.dynamic_index_in_dim(tokens, section_idx, 0, keepdims=False)
    own_grad = lax.dynamic_index_in_dim(out_grad, section_idx, 0, keepdims=False)

    hidden, kept_first = forward_layer(own_tokens, layer_params[0], doc_ext)
    final, kept_second = forward_layer(hidden, layer_params[1], doc_ext)
    grad_hidden, gin_second, gout_second, small_second, _ = backward_layer(
        own_grad, kept_second, layer_params[1], doc_ext, None
    )
    reduced_second = reduce_layer(gin_second, gout_second, section_idx)
    grad_tokens, gin_first, gout_first, small_first, reduced_second = backward_layer(
        grad_hidden.astype(BF16), kept_first, layer_params[0], doc_ext, reduced_second
    )
    reduced_first = reduce_layer(gin_first, gout_first, section_idx)

    mine = jnp.where(at_first, reduced_first, reduced_second)
    theirs = swapped(jnp.where(at_first, reduced_second, reduced_first))
    grad_in_weight, grad_out_weight = unpacked(
        jnp.where(at_first, mine, theirs)[None], jnp.where(at_first, theirs, mine)[None], width
    )
    grad_in_weight = grad_in_weight.astype(F32)
    grad_out_weight = grad_out_weight.astype(F32)

    def by_batch(first, second):
        mine = jnp.where(at_first, first, second)
        got = swapped(jnp.where(at_first, second, first))
        return jnp.stack([jnp.where(at_first, mine, got), jnp.where(at_first, got, mine)])

    outs = by_batch(hidden, final)
    in_grads = by_batch(grad_tokens, grad_hidden)

    flat_first, flat_second = (
        jnp.concatenate([item.reshape(groups, -1) for item in small], axis=1)
        for small in (small_first, small_second)
    )
    flat = jnp.where(at_first, flat_first, flat_second)
    flat = flat + swapped(jnp.where(at_first, flat_second, flat_first))
    flat = lax.psum_scatter(flat, "group", scatter_dimension=0, tiled=False)
    flat = lax.psum(flat, "replica")
    small_out = []
    start = 0
    for item in smalls:
        small_out.append(flat[start : start + item.size].reshape(item.shape))
        start += item.size
    return (
        outs[None],
        in_grads[None],
        small_out[0],
        grad_in_weight[None],
        small_out[1],
        small_out[2],
        small_out[3],
        small_out[4],
        small_out[5],
        small_out[6],
        grad_out_weight[None],
    )


def solution(mesh):
    return jax.shard_map(
        on_device,
        mesh=mesh,
        in_specs=(
            P(None, ("group", "replica"), None),
            P(None, ("group", "replica"), None),
            P(None, "group", None),
            P("section", "group"),
            P("section", "group", None),
            P("section", "group", None),
            P("section", "group"),
            P("section", "group"),
            P("section", "group"),
            P("section", "group"),
            P("section", "group"),
            P("section", "group", None),
        ),
        out_specs=(
            P("section", None, ("group", "replica"), None),
            P("section", None, ("group", "replica"), None),
            P("section", "group"),
            P("section", "group", None),
            P("section", "group", None),
            P("section", "group"),
            P("section", "group"),
            P("section", "group"),
            P("section", "group"),
            P("section", "group"),
            P("section", "group", None),
        ),
        check_vma=False,
    )
```
